256 devices in a mesh: grp: 8 (over x, y_hi), ing: 32 (over y_lo, z, core).
Axes of the slice: x: 4, y: 4 (y_hi: 2, y_lo: 2; y = y_hi * 2 + y_lo), z: 8, core: 2. Of those that a mesh axis runs over, the one named last changes fastest.
Arguments:
- image_emb: float32 [32768, 1152], P(('grp', 'ing')), may hold values from -22 to 22
- text_emb: float32 [32768, 1152], P(('grp', 'ing')), may hold values from -22 to 22
- logit_scale: float32 [1], replicated, may hold values from 5 to 15
- logit_bias: float32 [1], replicated, may hold values from -3 to -1
Outputs:
- row_loss: float32 [32768], P(('grp', 'ing'))
- image_grad: float32 [32768, 1152], P(('grp', 'ing'))
- text_grad: float32 [32768, 1152], P(('grp', 'ing'))
The draws below stay inside these ranges and needn't reach their ends.
All inputs are finite; a program needn't handle non-finite values.
Results may differ from the reference program's by a relative error of at most 0.005.
Values may be sent and summed in bfloat16 or wider, within the bound.
A program may use at most 128 MiB of HBM per device.

```python
import math
import jax
import jax.numpy as jnp
from jax import lax

EMBED = 1152
ROWS = 128
STEPS = 2
PAIRS = 32768
N_GRP = 8
N_ING = 32


def row_scales(key):
    return jnp.exp(jax.random.uniform(key, (PAIRS, 1), jnp.float32, math.log(0.5), math.log(5.0)))


def draw_image_emb(key, part):
    key = jax.random.fold_in(key, 1)
    first_key, second_key = jax.random.split(key)
    scales = row_scales(second_key)
    values = jax.random.truncated_normal(first_key, -4.0, 4.0, (PAIRS, EMBED), jnp.float32)
    return scales * values


def draw_text_emb(key, part):
    key = jax.random.fold_in(key, 2)
    first_key, second_key = jax.random.split(key)
    scales = row_scales(second_key)
    values = jax.random.truncated_normal(first_key, -4.0, 4.0, (PAIRS, EMBED), jnp.float32)
    return scales * values


def setup_inputs(seed: int = 0) -> dict:
    keys = jax.random.split(jax.random.key(seed), 5)
    return {
        "image_emb": draw_image_emb(jax.random.fold_in(keys[4], 71), 0),
        "text_emb": draw_text_emb(jax.random.fold_in(keys[4], 71), 0),
        "logit_scale": jnp.clip(jnp.exp(jax.random.uniform(keys[2], (1,), jnp.float32, math.log(5.0), math.log(15.0))), 5.0, 15.0),
        "logit_bias": jnp.clip(jax.random.uniform(keys[3], (1,), jnp.float32, -3.0, -1.0), -3.0, -1.0),
    }


EPSILON = 1e-06

def normalize(raw_rows):
    norms = jnp.sqrt(lax.optimization_barrier(jnp.sum(raw_rows * raw_rows, axis=1, keepdims=True)) + EPSILON)
    return (raw_rows / norms, norms)

def restore(unit_grad, unit_rows, norms):
    return (unit_grad - unit_rows * lax.optimization_barrier(jnp.sum(unit_rows * unit_grad, axis=1, keepdims=True))) / norms

def reference(image_emb, text_emb, logit_scale, logit_bias):
    unit_img, norm_img = normalize(image_emb)
    unit_txt, norm_txt = normalize(text_emb)
    image_low = unit_img.astype(jnp.bfloat16)
    text_low = unit_txt.astype(jnp.bfloat16)
    group_rows = ROWS * N_ING
    scale_value = logit_scale[0]
    bias_value = logit_bias[0]
    indices = jnp.arange(group_rows, dtype=jnp.int32)
    labels_own = jnp.where(indices[:, None] == indices[None, :], 1.0, -1.0).astype(jnp.float32)

    def per_group(text_acc, group_index):
        image_block = lax.dynamic_slice_in_dim(image_low, group_index * group_rows, group_rows, 0)
        losses = jnp.zeros((group_rows,), jnp.float32)
        image_acc = jnp.zeros((group_rows, EMBED), jnp.float32)
        for cycle_step in range(STEPS):
            owner = ((group_index - cycle_step) % N_GRP).astype(jnp.int32)
            text_block = lax.dynamic_slice_in_dim(text_low, owner * group_rows, group_rows, 0)
            logits = scale_value * jnp.dot(image_block, text_block.T, preferred_element_type=jnp.float32) + bias_value
            labels = labels_own if cycle_step == 0 else -1.0
            losses = losses + lax.optimization_barrier(jnp.sum(jax.nn.softplus(-labels * logits), axis=1))
            coefficient = (-labels * jax.nn.sigmoid(-labels * logits)).astype(jnp.bfloat16)
            image_acc = image_acc + jnp.dot(coefficient, text_block, preferred_element_type=jnp.float32)
            partial_sum = jnp.dot(coefficient.T, image_block, preferred_element_type=jnp.float32)
            previous = lax.dynamic_slice_in_dim(text_acc, owner * group_rows, group_rows, 0)
            text_acc = lax.dynamic_update_slice_in_dim(text_acc, previous + partial_sum, owner * group_rows, 0)
        return (text_acc, (losses, image_acc))
    text_acc, (losses, image_accs) = lax.scan(per_group, jnp.zeros((PAIRS, EMBED), jnp.float32), jnp.arange(N_GRP, dtype=jnp.int32))
    row_loss = losses.reshape(PAIRS) / (STEPS * group_rows)
    image_grad = restore(scale_value * image_accs.reshape(PAIRS, EMBED), unit_img, norm_img)
    text_grad = restore(scale_value * text_acc, unit_txt, norm_txt)
    return (row_loss, image_grad, text_grad)
```

```python
import functools

import jax
import jax.numpy as jnp
from jax import lax
from jax.experimental import pallas as pl
from jax.experimental.pallas import tpu as pltpu
from jax.sharding import PartitionSpec as P

STEPS = 2
EPSILON = 1e-06
MESH = pl.DeviceIdType.MESH
F32, BF16 = jnp.float32, jnp.bfloat16

CORES, RING = 2, 8
N_AG = 4
N_RS = 2
N_T = 2


def column_dot(left, right):
    return lax.dot_general(left, right, (((1,), (1,)), ((), ())), preferred_element_type=F32)


def kernel(
    image_ref, text_ref, scale_ref, bias_ref,
    loss_ref, image_grad_ref, text_grad_ref,
    img, txt, coef, coef_t, part, tgrad, racc, sacc, rloss, sloss, losses,
    sib_out, sib_in, yp_out, yp_in, back_out, back_in,
    unit_i, unit_t, norm_i, norm_t,
    ag_s, ag_r, t_s, t_r, f_s, rs_s, rs_r, l_s, l_r, sib_s, sib_r, yp_s, yp_r, bk_s, bk_r,
):
    rows, embed = image_ref.shape
    n_grp = lax.axis_size("grp")
    g, i = lax.axis_index("grp"), lax.axis_index("ing")
    core, z, y = i % CORES, (i // CORES) % RING, i // (CORES * RING)
    dz = 1 - 2 * core

    def device(group, y_, z_, core_):
        return (group, (y_ * RING + z_) * CORES + core_)

    nxt = device(g, y, lax.rem(z + dz + RING, RING), core)
    prv = device(g, y, lax.rem(z - dz + RING, RING), core)
    sib = device(g, y, z, 1 - core)
    ypart = device(g, 1 - y, z, core)
    ahead = device(lax.rem(g + 1, n_grp), 1 - y, z, core)
    behind = device(lax.rem(g + n_grp - 1, n_grp), 1 - y, z, core)

    barrier = pltpu.get_barrier_semaphore()
    for peer in (nxt, prv, sib, ypart, ahead, behind):
        pl.semaphore_signal(barrier, inc=1, device_id=peer, device_id_type=MESH)

    def send(src, dst, s_sem, r_sem, to):
        copy = pltpu.make_async_remote_copy(
            src_ref=src, dst_ref=dst, send_sem=s_sem, recv_sem=r_sem,
            device_id=to, device_id_type=MESH,
        )
        copy.start()
        sent.append(copy)

    def landed(dst, r_sem):
        pltpu.make_async_remote_copy(
            src_ref=dst, dst_ref=dst, send_sem=r_sem, recv_sem=r_sem,
            device_id=nxt, device_id_type=MESH,
        ).wait_recv()

    sent = []

    def normalize(raw_ref, unit, norm, low):
        raw = raw_ref[...]
        norms = jnp.sqrt(jnp.sum(raw * raw, axis=1, keepdims=True) + EPSILON)
        units = raw / norms
        unit[...] = units
        norm[...] = norms
        low[...] = units.astype(BF16)

    def img_rows(slot, c):
        n = rows // N_AG
        return img.at[pl.ds(slot * rows + c * n, n)]

    def ring_on(slot):
        for c in range(N_AG):
            if slot < RING - 1:
                landed(img_rows(slot, c), ag_r.at[slot, c])
            to = (slot + 1) % RING
            if to < RING - 1:
                send(img_rows(slot, c), img_rows(to, c), ag_s.at[to, c], ag_r.at[to, c], nxt)

    def t_rows(slot, c):
        n = rows // N_T
        return txt.at[pl.ds(slot * rows + c * n, n)]

    def t_send(slot, c, to_slot, sem, to):
        send(t_rows(slot, c), t_rows(to_slot, c), f_s.at[sem, c], t_r.at[to_slot, c], to)

    def t_landed(slot, c):
        landed(t_rows(slot, c), t_r.at[slot, c])

    normalize(image_ref, unit_i, norm_i, img.at[pl.ds((RING - 1) * rows, rows)])
    pl.semaphore_wait(barrier, 6)
    ring_on(RING - 1)
    normalize(text_ref, unit_t, norm_t, txt.at[pl.ds(0, rows)])
    for c in range(N_T):
        t_send(0, c, 2, 0, ahead)
        t_send(0, c, 1, 1, ypart)
        t_send(0, c, 4, 2, sib)

    ring_on(0)
    for c in range(N_T):
        t_landed(1, c)
        if c == 0:
            t_send(1, c, 3, 3, ahead)
        t_send(1, c, 5, 4, sib)
        t_landed(2, c)
        if c == 1:
            t_send(2, c, 3, 3, ypart)
        t_send(2, c, 6, 5, sib)
    ring_on(1)
    ring_on(2)
    for c in range(N_T):
        t_landed(3, c)
        t_send(3, c, 7, 6, sib)
    ring_on(3)
    for slot in range(4, 8):
        for c in range(N_T):
            t_landed(slot, c)

    scale, bias = scale_ref[0], bias_ref[0]
    wide = 2 * rows
    blocks = 8 * rows // wide
    apart = lax.broadcasted_iota(jnp.int32, (wide, wide), 1) - lax.broadcasted_iota(
        jnp.int32, (wide, wide), 0
    )

    def score(u):
        def block(b, total):
            at = pl.ds(pl.multiple_of(b * wide, wide), wide)
            x = scale * column_dot(txt[at, :], img[pl.ds(u * wide, wide), :]) + bias
            own = apart == (7 * rows - u * wide) + b * wide
            m = jnp.where(own, -x, x)
            e = jnp.exp(-jnp.abs(m))
            one = 1.0 + e
            inv = 1.0 / one
            log1p = jnp.log(one) + (e - (one - 1.0)) * inv
            total = total + jnp.sum(jnp.maximum(m, 0.0) + log1p, axis=0, keepdims=True)
            sig = jnp.where(m >= 0.0, inv, e * inv)
            cf = jnp.where(own, -sig, sig).astype(BF16)
            coef[at, :] = cf
            coef_t[:, at] = cf.T
            return total

        losses[:, pl.ds(u * wide, wide)] = lax.fori_loop(
            0, blocks, block, jnp.zeros((1, wide), F32)
        )

    def image_part(u):
        step = 3 * 128

        def tile(n, carry):
            at = pl.ds(pl.multiple_of(n * step, step), step)
            part[pl.ds(u * wide, wide), at] = jnp.dot(
                coef_t[...], txt[:, at], preferred_element_type=F32
            )
            return carry

        lax.fori_loop(0, embed // step, tile, 0)

    def text_part(u):
        def block(b, carry):
            at = pl.ds(pl.multiple_of(b * wide, wide), wide)
            add = jnp.dot(coef[at, :], img[pl.ds(u * wide, wide), :], preferred_element_type=F32)
            tgrad[at, :] = add if u == 0 else tgrad[at, :] + add
            return carry

        lax.fori_loop(0, blocks, block, 0)

    def sum_on(slot):
        mine = losses[:, pl.ds(slot * rows, rows)]
        if slot > 0:
            landed(rloss.at[slot - 1], l_r.at[slot - 1])
            mine = mine + rloss[slot - 1, 0:1, :]
        sloss[slot] = jnp.broadcast_to(mine, (8, rows))
        send(sloss.at[slot], rloss.at[slot], l_s.at[slot], l_r.at[slot], nxt)
        n = rows // N_RS
        for c in range(N_RS):
            at = pl.ds(c * n, n)
            value = part[pl.ds(slot * rows + c * n, n), :]
            if slot > 0:
                landed(racc.at[slot - 1, at], rs_r.at[slot - 1, c])
                value = value + racc[slot - 1, at, :].astype(F32)
            sacc[slot, at, :] = value.astype(BF16)
            send(sacc.at[slot, at], racc.at[slot, at], rs_s.at[slot, c], rs_r.at[slot, c], nxt)

    def shard(slot):
        return pl.ds(slot * rows, rows)

    score(0)
    image_part(0)
    sum_on(0)
    text_part(0)
    ring_on(4)
    score(1)
    image_part(1)
    sum_on(1)
    text_part(1)
    ring_on(5)
    score(2)
    image_part(2)
    sum_on(2)
    text_part(2)
    ring_on(6)
    score(3)
    text_part(3)
    for s in (2, 3, 0, 1):
        sib_out[s] = tgrad[shard(4 + s), :].astype(BF16)
        send(sib_out.at[s], sib_in.at[s], sib_s.at[s], sib_r.at[s], sib)
    sum_on(3)
    image_part(3)

    def from_sib(s):
        landed(sib_in.at[s], sib_r.at[s])
        tgrad[shard(s), :] = tgrad[shard(s), :] + sib_in[s].astype(F32)

    def to_partner(s, n):
        from_sib(s)
        yp_out[n] = tgrad[shard(s), :].astype(BF16)
        send(yp_out.at[n], yp_in.at[n], yp_s.at[n], yp_r.at[n], ypart)

    to_partner(3, 0)
    to_partner(1, 1)
    from_sib(2)
    from_sib(0)
    sum_on(4)
    landed(yp_in.at[0], yp_r.at[0])
    back_out[...] = (tgrad[shard(2), :] + yp_in[0].astype(F32)).astype(BF16)
    send(back_out, back_in, bk_s, bk_r, behind)
    sum_on(5)
    landed(yp_in.at[1], yp_r.at[1])
    tgrad[shard(0), :] = tgrad[shard(0), :] + yp_in[1].astype(F32)

    def restore(unit_grad, unit, norm):
        units = unit[...]
        return (unit_grad - units * jnp.sum(units * unit_grad, axis=1, keepdims=True)) / norm[...]

    sum_on(6)
    landed(back_in, bk_r)
    text_grad_ref[...] = restore(
        scale * (tgrad[shard(0), :] + back_in[...].astype(F32)), unit_t, norm_t
    )

    landed(rloss.at[6], l_r.at[6])
    n_scored = STEPS * rows * lax.axis_size("ing")
    loss_ref[...] = (losses[:, shard(7)] + rloss[6, 0:1, :]) / n_scored
    n = rows // N_RS
    for c in range(N_RS):
        landed(racc.at[6, pl.ds(c * n, n)], rs_r.at[6, c])
    image_grad_ref[...] = restore(
        scale * (part[shard(7), :] + racc[6].astype(F32)), unit_i, norm_i
    )
    for copy in sent:
        copy.wait_send()


def on_device(image_emb, text_emb, logit_scale, logit_bias):
    rows, embed = image_emb.shape
    full, dma = RING * rows, pltpu.SemaphoreType.DMA
    wide = 2 * rows
    vmem, smem = pl.BlockSpec(memory_space=pltpu.VMEM), pl.BlockSpec(memory_space=pltpu.SMEM)
    loss, image_grad, text_grad = pl.pallas_call(
        kernel,
        out_shape=(
            jax.ShapeDtypeStruct((1, rows), F32),
            jax.ShapeDtypeStruct((rows, embed), F32),
            jax.ShapeDtypeStruct((rows, embed), F32),
        ),
        in_specs=[vmem, vmem, smem, smem],
        out_specs=(vmem, vmem, vmem),
        scratch_shapes=[
            pltpu.VMEM((full, embed), BF16),
            pltpu.VMEM((full, embed), BF16),
            pltpu.VMEM((full, wide), BF16),
            pltpu.VMEM((wide, full), BF16),
            pltpu.VMEM((full, embed), F32),
            pltpu.VMEM((full, embed), F32),
            pltpu.VMEM((7, rows, embed), BF16),
            pltpu.VMEM((7, rows, embed), BF16),
            pltpu.VMEM((7, 8, rows), F32),
            pltpu.VMEM((7, 8, rows), F32),
            pltpu.VMEM((1, full), F32),
            pltpu.VMEM((4, rows, embed), BF16),
            pltpu.VMEM((4, rows, embed), BF16),
            pltpu.VMEM((2, rows, embed), BF16),
            pltpu.VMEM((2, rows, embed), BF16),
            pltpu.VMEM((rows, embed), BF16),
            pltpu.VMEM((rows, embed), BF16),
            pltpu.VMEM((rows, embed), F32),
            pltpu.VMEM((rows, embed), F32),
            pltpu.VMEM((rows, 1), F32),
            pltpu.VMEM((rows, 1), F32),
            dma((7, N_AG)), dma((7, N_AG)),
            dma((8, N_T)), dma((8, N_T)), dma((7, N_T)),
            dma((7, N_RS)), dma((7, N_RS)),
            dma((7,)), dma((7,)),
            dma((4,)), dma((4,)),
            dma((2,)), dma((2,)),
            dma, dma,
        ],
        compiler_params=pltpu.CompilerParams(
            collective_id=0, has_side_effects=True, vmem_limit_bytes=56 * 2**20
        ),
        cost_estimate=pl.CostEstimate(
            flops=6 * full * full * embed, bytes_accessed=16 * rows * embed, transcendentals=3 * full * full
        ),
    )(image_emb, text_emb, logit_scale, logit_bias)
    return loss.reshape(rows), image_grad, text_grad


def solution(mesh):
    placed = (P(("grp", "ing"), None), P(("grp", "ing"), None), P(), P())
    return jax.shard_map(
        on_device,
        mesh=mesh,
        in_specs=placed,
        out_specs=(P(("grp", "ing")), P(("grp", "ing"), None), P(("grp", "ing"), None)),
        check_vma=False,
    )
```

```python
import jax
import jax.numpy as jnp
from jax import lax
from jax.experimental import pallas as pl
from jax.experimental.pallas import tpu as pltpu
from jax.sharding import PartitionSpec as P

STEPS = 2
EPSILON = 1e-06
MESH = pl.DeviceIdType.MESH
F32, BF16 = jnp.float32, jnp.bfloat16

CORES, RING = 2, 8
N_AG = 2
N_RS = 4
N_T = 4
SLOT = {1: 0, 7: 1, 2: 2, 6: 3, 3: 4, 5: 5, 4: 6, 0: 7}
TURN = 4
LANDS = {hop: n for n, hop in enumerate([*range(TURN + 1, RING + 1), *range(TURN - 1)])}


def column_dot(left, right):
    return lax.dot_general(left, right, (((1,), (1,)), ((), ())), preferred_element_type=F32)


def row_norms(raw):
    return jnp.sqrt(jnp.sum(raw * raw, axis=1, keepdims=True) + EPSILON)


def kernel(
    image_ref, text_ref, scale_ref, bias_ref,
    loss_ref, image_sum_ref, text_sum_ref,
    raw_i, raw_t, img, txt, coef, part, tgrad, racc, sacc, rloss, sloss, losses,
    sib_out, sib_in, d_out, d_in,
    in_sem, ag_s, ag_r, t_r, f_s, rs_s, rs_r, l_s, l_r, sib_s, sib_r, d_s, d_r,
):
    rows, embed = raw_i.shape
    n_grp = lax.axis_size("grp")
    g, i = lax.axis_index("grp"), lax.axis_index("ing")
    core, z, y = i % CORES, (i // CORES) % RING, i // (CORES * RING)
    dz = 1 - 2 * core

    def device(group, y_, z_, core_):
        return (group, (y_ * RING + z_) * CORES + core_)

    nxt = device(g, y, lax.rem(z + dz + RING, RING), core)
    prv = device(g, y, lax.rem(z - dz + RING, RING), core)
    sib = device(g, y, z, 1 - core)
    ypart = device(g, 1 - y, z, core)
    ahead = device(lax.rem(g + 1, n_grp), 1 - y, z, core)
    behind = device(lax.rem(g + n_grp - 1, n_grp), 1 - y, z, core)

    barrier = pltpu.get_barrier_semaphore()
    for peer in (nxt, prv, sib, ypart, ahead, behind):
        pl.semaphore_signal(barrier, inc=1, device_id=peer, device_id_type=MESH)
    fetch_i = pltpu.make_async_copy(image_ref, raw_i, in_sem.at[0])
    fetch_t = pltpu.make_async_copy(text_ref, raw_t, in_sem.at[1])
    fetch_i.start()
    fetch_t.start()

    sent = []

    def send(src, dst, s_sem, r_sem, to):
        copy = pltpu.make_async_remote_copy(
            src_ref=src, dst_ref=dst, send_sem=s_sem, recv_sem=r_sem,
            device_id=to, device_id_type=MESH,
        )
        copy.start()
        sent.append(copy)

    def landed(dst, sem):
        pltpu.make_async_remote_copy(
            src_ref=dst, dst_ref=dst, send_sem=sem, recv_sem=sem,
            device_id=nxt, device_id_type=MESH,
        ).wait_recv()

    def img_rows(hop, c):
        n = rows // N_AG
        return img.at[pl.ds(SLOT[hop] * rows + c * n, n)]

    def ring_send(hop, to, c, peer):
        send(img_rows(hop, c), img_rows(to, c), ag_s.at[to - 1, c], ag_r.at[to - 1, c], peer)

    def ring_chunk(hop, c):
        landed(img_rows(hop, c), ag_r.at[hop - 1, c])
        if hop < RING // 2:
            ring_send(hop, hop + 1, c, nxt)
        elif hop > RING // 2 + 1:
            ring_send(hop, hop - 1, c, prv)

    def t_rows(slot, c):
        n = rows // N_T
        return txt.at[pl.ds(slot * rows + c * n, n)]

    def t_send(slot, c, to_slot, sem, to):
        send(t_rows(slot, c), t_rows(to_slot, c), f_s.at[sem, c], t_r.at[to_slot, c], to)

    def t_landed(slot, c):
        landed(t_rows(slot, c), t_r.at[slot, c])

    def normalize(raw_ref, low):
        raw = raw_ref[...]
        low[...] = (raw / row_norms(raw)).astype(BF16)

    scale, bias = scale_ref[0], bias_ref[0]
    wide = 2 * rows

    def images(u):
        return pl.ds(u * wide, wide)

    def score(u):
        dots = column_dot(txt[...], img[images(u), :])
        x = scale * dots + bias
        e = jnp.exp(x)
        one = 1.0 + e
        inv = pl.reciprocal(one, approx=True)
        inv = inv * (2.0 - one * inv)
        loss = jnp.log(one) + (e - (one - 1.0)) * inv
        coef[u] = (e * inv).astype(BF16)
        losses[:, images(u)] = jnp.sum(loss, axis=0, keepdims=True)
        if u == 3:
            x = x[:rows, rows:]
            own = lax.broadcasted_iota(jnp.int32, x.shape, 0) == lax.broadcasted_iota(
                jnp.int32, x.shape, 1
            )
            m = jnp.exp(-jnp.abs(x))
            one_m = 1.0 + m
            pair = jnp.log(one_m) + (m - (one_m - 1.0)) / one_m + jnp.maximum(-x, 0.0)
            inv = inv[:rows, rows:]
            coef[u, :rows, rows:] = jnp.where(own, -inv, e[:rows, rows:] * inv).astype(BF16)
            loss = jnp.concatenate(
                [jnp.where(own, pair, loss[:rows, rows:]), loss[rows:, rows:]], axis=0
            )
            losses[:, pl.ds(7 * rows, rows)] = jnp.sum(loss, axis=0, keepdims=True)

    def image_part(u):
        part[images(u), :] = lax.dot_general(
            coef[u], txt[...], (((0,), (0,)), ((), ())), preferred_element_type=F32
        )

    def text_part(u, first):
        add = jnp.dot(coef[u], img[images(u), :], preferred_element_type=F32)
        tgrad[...] = add if first else tgrad[...] + add

    def sum_on(hop, c):
        slot = SLOT[hop]
        to, peer = (hop + 1, nxt) if hop >= TURN else (hop - 1, prv)
        into, came = LANDS[to], LANDS.get(hop)
        n = rows // N_RS
        at = pl.ds(c * n, n)
        value = part[pl.ds(slot * rows + c * n, n), :]
        if came is not None:
            landed(racc.at[came, at], rs_r.at[came, c])
            value = value + racc[came, at, :].astype(F32)
        sacc[slot, at, :] = value.astype(BF16)
        send(sacc.at[slot, at], racc.at[into, at], rs_s.at[slot, c], rs_r.at[into, c], peer)
        if c == 0:
            mine = losses[:, pl.ds(slot * rows, rows)]
            if came is not None:
                landed(rloss.at[came], l_r.at[came])
                mine = mine + rloss[came, 0:1, :]
            sloss[slot] = jnp.broadcast_to(mine, (8, rows))
            send(sloss.at[slot], rloss.at[into], l_s.at[slot], l_r.at[into], peer)

    def sums_on(hop):
        for c in range(N_RS):
            sum_on(hop, c)

    half = rows // 2

    def to_sib(s):
        sib_out[s] = tgrad[pl.ds((4 + s) * rows, rows), :].astype(BF16)
        send(sib_out.at[s], sib_in.at[s], sib_s.at[s], sib_r.at[s], sib)

    def from_sib(s):
        landed(sib_in.at[s], sib_r.at[s])
        at = pl.ds(s * rows, rows)
        tgrad[at, :] = tgrad[at, :] + sib_in[s].astype(F32)

    def t_half(s, h):
        return pl.ds(s * rows + h * half, half)

    def d_send(m, s, h, to):
        d_out[m] = tgrad[t_half(s, h), :].astype(BF16)
        send(d_out.at[m], d_in.at[m], d_s.at[m], d_r.at[m], to)

    def d_add(m, s, h):
        landed(d_in.at[m], d_r.at[m])
        at = t_half(s, h)
        tgrad[at, :] = tgrad[at, :] + d_in[m].astype(F32)

    fetch_i.wait()
    normalize(raw_i, img.at[pl.ds((RING - 1) * rows, rows)])
    pl.semaphore_wait(barrier, 6)
    for c in range(N_AG):
        ring_send(0, 1, c, nxt)
        ring_send(0, 7, c, prv)
    fetch_t.wait()
    normalize(raw_t, txt.at[pl.ds(0, rows)])
    for c in range(N_T):
        t_send(0, c, 1, 1, ypart)
        t_send(0, (c + 2) % N_T, 2, 0, ahead)
    for c in range(N_T):
        t_send(0, c, 4, 2, sib)

    def ring_on(hop, back, c):
        ring_chunk(hop, c)
        ring_chunk(back, c)

    def partner_text(c):
        t_landed(1, c)
        if c < 2:
            t_send(1, c, 3, 3, ahead)
        t_send(1, c, 5, 4, sib)

    def behind_text(c):
        t_landed(2, c)
        if c >= 2:
            t_send(2, c, 3, 3, ypart)
        t_send(2, c, 6, 5, sib)

    def far_text(c):
        t_landed(3, c)
        t_send(3, c, 7, 6, sib)

    partner_text(0)
    behind_text(2)
    partner_text(1)
    ring_on(1, 7, 0)
    behind_text(3)
    partner_text(2)
    behind_text(0)
    partner_text(3)
    ring_on(1, 7, 1)
    behind_text(1)
    far_text(2)
    far_text(0)
    far_text(3)
    ring_on(2, 6, 0)
    far_text(1)
    for slot in range(4, 8):
        for c in range(N_T):
            t_landed(slot, c)
    score(0)
    ring_on(2, 6, 1)
    score(1)
    image_part(1)
    ring_on(3, 5, 0)
    text_part(1, True)
    image_part(0)
    text_part(0, False)
    ring_on(3, 5, 1)
    score(2)
    image_part(2)
    sums_on(3)
    ring_chunk(4, 0)
    ring_chunk(4, 1)
    score(3)
    image_part(3)
    sums_on(4)
    text_part(2, False)
    text_part(3, False)
    for s in (3, 2, 1, 0):
        to_sib(s)
    sums_on(2)
    sums_on(5)
    from_sib(3)
    d_send(0, 3, 0, behind)
    d_send(1, 3, 1, ypart)
    from_sib(2)
    d_send(2, 2, 0, behind)
    from_sib(1)
    d_send(3, 1, 1, ypart)
    from_sib(0)
    sums_on(1)
    d_add(1, 2, 1)
    d_send(4, 2, 1, behind)
    sums_on(6)
    d_add(0, 1, 0)
    d_send(5, 1, 0, ypart)
    d_add(3, 0, 1)
    d_add(2, 0, 0)
    sums_on(7)
    d_add(5, 0, 0)
    d_add(4, 0, 1)
    text_sum_ref[...] = tgrad[pl.ds(0, rows), :]

    mine = losses[:, pl.ds(7 * rows, rows)]
    for came in (LANDS[0], LANDS[8]):
        landed(rloss.at[came], l_r.at[came])
        mine = mine + rloss[came, 0:1, :]
    loss_ref[...] = mine
    n = rows // N_RS
    for c in range(N_RS):
        at = pl.ds(c * n, n)
        value = part[pl.ds(7 * rows + c * n, n), :]
        for came in (LANDS[0], LANDS[8]):
            landed(racc.at[came, at], rs_r.at[came, c])
            value = value + racc[came, at, :].astype(F32)
        image_sum_ref[at, :] = value
    for copy in sent:
        copy.wait_send()


def finish(scored, image_ref, text_ref, image_sum_ref, text_sum_ref, loss_sum_ref, scale_ref,
           loss_ref, image_grad_ref, text_grad_ref):
    scale = scale_ref[0]

    def restore(raw_ref, sum_ref, out_ref):
        raw = raw_ref[...]
        norms = row_norms(raw)
        units = raw / norms
        grad = scale * sum_ref[...]
        out_ref[...] = (grad - units * jnp.sum(units * grad, axis=1, keepdims=True)) / norms

    restore(image_ref, image_sum_ref, image_grad_ref)
    restore(text_ref, text_sum_ref, text_grad_ref)

    @pl.when(pl.program_id(0) == 0)
    def _():
        loss_ref[...] = loss_sum_ref[0, :] / scored


def on_device(image_emb, text_emb, logit_scale, logit_bias):
    rows, embed = image_emb.shape
    full, dma = RING * rows, pltpu.SemaphoreType.DMA
    wide, half = 2 * rows, rows // 2
    whole, smem = pl.BlockSpec(memory_space=pltpu.VMEM), pl.BlockSpec(memory_space=pltpu.SMEM)
    far = pl.BlockSpec(memory_space=pl.ANY)
    vmem = pltpu.VMEM
    loss_sum, image_sum, text_sum = pl.pallas_call(
        kernel,
        out_shape=(
            jax.ShapeDtypeStruct((1, rows), F32),
            jax.ShapeDtypeStruct((rows, embed), F32),
            jax.ShapeDtypeStruct((rows, embed), F32),
        ),
        in_specs=[far, far, smem, smem],
        out_specs=(whole, whole, whole),
        scratch_shapes=[
            vmem((rows, embed), F32),
            vmem((rows, embed), F32),
            vmem((full, embed), BF16),
            vmem((full, embed), BF16),
            vmem((4, full, wide), BF16),
            vmem((full, embed), F32),
            vmem((full, embed), F32),
            vmem((7, rows, embed), BF16),
            vmem((7, rows, embed), BF16),
            vmem((7, 8, rows), F32),
            vmem((7, 8, rows), F32),
            vmem((1, full), F32),
            vmem((4, rows, embed), BF16),
            vmem((4, rows, embed), BF16),
            vmem((6, half, embed), BF16),
            vmem((6, half, embed), BF16),
            dma((2,)),
            dma((7, N_AG)), dma((7, N_AG)),
            dma((8, N_T)), dma((7, N_T)),
            dma((7, N_RS)), dma((7, N_RS)),
            dma((7,)), dma((7,)),
            dma((4,)), dma((4,)),
            dma((6,)), dma((6,)),
        ],
        compiler_params=pltpu.CompilerParams(
            collective_id=0, has_side_effects=True, vmem_limit_bytes=56 * 2**20
        ),
        cost_estimate=pl.CostEstimate(
            flops=6 * full * full * embed, bytes_accessed=16 * rows * embed, transcendentals=3 * full * full
        ),
    )(image_emb, text_emb, logit_scale, logit_bias)
    n_cut = 1
    tile = pl.BlockSpec((rows // n_cut, embed), lambda n: (n, 0))
    scored = STEPS * rows * lax.axis_size("ing")
    return pl.pallas_call(
        lambda *refs: finish(scored, *refs),
        grid=(n_cut,),
        out_shape=(
            jax.ShapeDtypeStruct((rows,), F32),
            jax.ShapeDtypeStruct((rows, embed), F32),
            jax.ShapeDtypeStruct((rows, embed), F32),
        ),
        in_specs=[tile, tile, tile, tile, pl.BlockSpec((1, rows), lambda n: (0, 0)), smem],
        out_specs=(pl.BlockSpec((rows,), lambda n: (0,)), tile, tile),
    )(image_emb, text_emb, image_sum, text_sum, loss_sum, logit_scale)


def solution(mesh):
    placed = (P(("grp", "ing"), None), P(("grp", "ing"), None), P(), P())
    return jax.shard_map(
        on_device,
        mesh=mesh,
        in_specs=placed,
        out_specs=(P(("grp", "ing")), P(("grp", "ing"), None), P(("grp", "ing"), None)),
        check_vma=False,
    )
```

```python
import jax
import jax.numpy as jnp
from jax import lax
from jax.experimental import pallas as pl
from jax.experimental.pallas import tpu as pltpu
from jax.sharding import PartitionSpec as P

STEPS = 2
EPSILON = 1e-06
MESH = pl.DeviceIdType.MESH
F32, BF16 = jnp.float32, jnp.bfloat16

CORES, RING = 2, 8
N_AG = 2
N_T = 4
SLOT = {1: 0, 7: 1, 2: 2, 6: 3, 3: 4, 5: 5, 4: 6, 0: 7}
TURNS = (4, 4, 4, 4)
N_RS = len(TURNS)


def column_dot(left, right):
    return lax.dot_general(left, right, (((1,), (1,)), ((), ())), preferred_element_type=F32)


def row_norms(raw):
    return jnp.sqrt(jnp.sum(raw * raw, axis=1, keepdims=True) + EPSILON)


def kernel(
    image_ref, text_ref, scale_ref, bias_ref,
    loss_ref, image_grad_ref, text_grad_ref,
    scalars, raw_i, raw_t, norm_i, norm_t, img, txt, coef, part, tgrad, racc, sacc, rloss, sloss, losses,
    sib_out, sib_in, d_out, d_in,
    in_sem, out_sem, ag_s, ag_r, t_r, f_s, rs_s, rs_r, l_s, l_r, sib_s, sib_r, d_s, d_r,
):
    rows, embed = raw_i.shape
    n_grp = lax.axis_size("grp")
    g, i = lax.axis_index("grp"), lax.axis_index("ing")
    core, z, y = i % CORES, (i // CORES) % RING, i // (CORES * RING)
    dz = 1 - 2 * core

    def device(group, y_, z_, core_):
        return (group, (y_ * RING + z_) * CORES + core_)

    nxt = device(g, y, lax.rem(z + dz + RING, RING), core)
    prv = device(g, y, lax.rem(z - dz + RING, RING), core)
    sib = device(g, y, z, 1 - core)
    ypart = device(g, 1 - y, z, core)
    ahead = device(lax.rem(g + 1, n_grp), 1 - y, z, core)
    behind = device(lax.rem(g + n_grp - 1, n_grp), 1 - y, z, core)

    barrier = pltpu.get_barrier_semaphore()
    for peer in (nxt, prv, sib, ypart, ahead, behind):
        pl.semaphore_signal(barrier, inc=1, device_id=peer, device_id_type=MESH)

    def fetch(src, dst, n):
        copy = pltpu.make_async_copy(src, dst, in_sem.at[n])
        copy.start()
        return copy

    n_ag = rows // N_AG
    fetch_i = [
        fetch(image_ref.at[pl.ds(c * n_ag, n_ag)], raw_i.at[pl.ds(c * n_ag, n_ag)], c)
        for c in range(N_AG)
    ]
    fetch_t = fetch(text_ref, raw_t, N_AG)
    fetch_s = [
        fetch(scale_ref, scalars.at[0], N_AG + 1), fetch(bias_ref, scalars.at[1], N_AG + 2)
    ]

    sent = []

    def send(src, dst, s_sem, r_sem, to):
        copy = pltpu.make_async_remote_copy(
            src_ref=src, dst_ref=dst, send_sem=s_sem, recv_sem=r_sem,
            device_id=to, device_id_type=MESH,
        )
        copy.start()
        sent.append(copy)

    def landed(dst, sem):
        pltpu.make_async_remote_copy(
            src_ref=dst, dst_ref=dst, send_sem=sem, recv_sem=sem,
            device_id=nxt, device_id_type=MESH,
        ).wait_recv()

    def img_rows(hop, c):
        n = rows // N_AG
        return img.at[pl.ds(SLOT[hop] * rows + c * n, n)]

    def ring_send(hop, to, c, peer):
        send(img_rows(hop, c), img_rows(to, c), ag_s.at[to - 1, c], ag_r.at[to - 1, c], peer)

    def ring_chunk(hop, c):
        landed(img_rows(hop, c), ag_r.at[hop - 1, c])
        if hop < RING // 2:
            ring_send(hop, hop + 1, c, nxt)
        elif hop > RING // 2 + 1:
            ring_send(hop, hop - 1, c, prv)

    def t_rows(slot, c):
        n = rows // N_T
        return txt.at[pl.ds(slot * rows + c * n, n)]

    def t_send(slot, c, to_slot, sem, to):
        send(t_rows(slot, c), t_rows(to_slot, c), f_s.at[sem, c], t_r.at[to_slot, c], to)

    def t_landed(slot, c):
        landed(t_rows(slot, c), t_r.at[slot, c])

    def normalize(raw_ref, norm_ref, low):
        raw = raw_ref[...]
        norms = row_norms(raw)
        norm_ref[...] = norms
        low[...] = (raw / norms).astype(BF16)

    def restore(raw_ref, norm_ref, at, unit_grad):
        norms = norm_ref[at, :]
        units = raw_ref[at, :] / norms
        grad = scale * unit_grad
        raw_ref[at, :] = (grad - units * jnp.sum(units * grad, axis=1, keepdims=True)) / norms

    wide = 2 * rows

    def images(u):
        return pl.ds(u * wide, wide)

    def score(u):
        dots = column_dot(txt[...], img[images(u), :])
        x = scale * dots + bias
        e = jnp.exp(x)
        one = 1.0 + e
        inv = pl.reciprocal(one, approx=True)
        inv = inv * (2.0 - one * inv)
        loss = jnp.log(one) + (e - (one - 1.0)) * inv
        coef[u] = (e * inv).astype(BF16)
        losses[:, images(u)] = jnp.sum(loss, axis=0, keepdims=True)
        if u == 3:
            x = x[:rows, rows:]
            own = lax.broadcasted_iota(jnp.int32, x.shape, 0) == lax.broadcasted_iota(
                jnp.int32, x.shape, 1
            )
            m = jnp.exp(-jnp.abs(x))
            one_m = 1.0 + m
            pair = jnp.log(one_m) + (m - (one_m - 1.0)) / one_m + jnp.maximum(-x, 0.0)
            inv = inv[:rows, rows:]
            coef[u, :rows, rows:] = jnp.where(own, -inv, e[:rows, rows:] * inv).astype(BF16)
            loss = jnp.concatenate(
                [jnp.where(own, pair, loss[:rows, rows:]), loss[rows:, rows:]], axis=0
            )
            losses[:, pl.ds(7 * rows, rows)] = jnp.sum(loss, axis=0, keepdims=True)

    def image_part(u):
        part[images(u), :] = lax.dot_general(
            coef[u], txt[...], (((0,), (0,)), ((), ())), preferred_element_type=F32
        )

    def text_part(u, first):
        add = jnp.dot(coef[u], img[images(u), :], preferred_element_type=F32)
        tgrad[...] = add if first else tgrad[...] + add

    def sum_on(hop, c):
        slot = SLOT[hop]
        to, peer = (hop + 1, nxt) if hop >= TURNS[c] else (hop - 1, prv)
        starts = hop in (TURNS[c], TURNS[c] - 1)
        n = rows // N_RS
        at = pl.ds(c * n, n)
        value = part[pl.ds(slot * rows + c * n, n), :]
        if not starts:
            landed(racc.at[hop, at], rs_r.at[hop, c])
            value = value + racc[hop, at, :].astype(F32)
        sacc[slot, at, :] = value.astype(BF16)
        send(sacc.at[slot, at], racc.at[to, at], rs_s.at[slot, c], rs_r.at[to, c], peer)
        if c == 0:
            mine = losses[:, pl.ds(slot * rows, rows)]
            if not starts:
                landed(rloss.at[hop], l_r.at[hop])
                mine = mine + rloss[hop, 0:1, :]
            sloss[slot] = jnp.broadcast_to(mine, (8, rows))
            send(sloss.at[slot], rloss.at[to], l_s.at[slot], l_r.at[to], peer)

    def ends(c):
        return (0, RING) if TURNS[c] > 1 else (RING,)

    half = rows // 2

    def to_sib(s):
        sib_out[s] = tgrad[pl.ds((4 + s) * rows, rows), :].astype(BF16)
        send(sib_out.at[s], sib_in.at[s], sib_s.at[s], sib_r.at[s], sib)

    def from_sib(s):
        landed(sib_in.at[s], sib_r.at[s])
        at = pl.ds(s * rows, rows)
        tgrad[at, :] = tgrad[at, :] + sib_in[s].astype(F32)

    def t_half(s, h):
        return pl.ds(s * rows + h * half, half)

    def d_send(m, s, h, to):
        d_out[m] = tgrad[t_half(s, h), :].astype(BF16)
        send(d_out.at[m], d_in.at[m], d_s.at[m], d_r.at[m], to)

    def d_add(m, s, h):
        landed(d_in.at[m], d_r.at[m])
        at = t_half(s, h)
        tgrad[at, :] = tgrad[at, :] + d_in[m].astype(F32)

    for c in range(N_AG):
        fetch_i[c].wait()
        at = pl.ds(c * n_ag, n_ag)
        normalize(raw_i.at[at], norm_i.at[at], img_rows(0, c))
        if c == 0:
            pl.semaphore_wait(barrier, 6)
        ring_send(0, 1, c, nxt)
        ring_send(0, 7, c, prv)
    fetch_t.wait()
    normalize(raw_t, norm_t, txt.at[pl.ds(0, rows)])
    for c in range(N_T):
        t_send(0, c, 1, 1, ypart)
        t_send(0, (c + 2) % N_T, 2, 0, ahead)
    for c in range(N_T):
        t_send(0, c, 4, 2, sib)
    for copy in fetch_s:
        copy.wait()
    scale, bias = scalars[0, 0], scalars[1, 0]

    def ring_on(hop, back, c):
        ring_chunk(hop, c)
        ring_chunk(back, c)

    def partner_text(c):
        t_landed(1, c)
        if c < 2:
            t_send(1, c, 3, 3, ahead)
        t_send(1, c, 5, 4, sib)

    def behind_text(c):
        t_landed(2, c)
        if c >= 2:
            t_send(2, c, 3, 3, ypart)
        t_send(2, c, 6, 5, sib)

    def far_text(c):
        t_landed(3, c)
        t_send(3, c, 7, 6, sib)

    partner_text(0)
    behind_text(2)
    partner_text(1)
    ring_on(1, 7, 0)
    behind_text(3)
    partner_text(2)
    behind_text(0)
    partner_text(3)
    ring_on(1, 7, 1)
    behind_text(1)
    far_text(2)
    far_text(0)
    far_text(3)
    ring_on(2, 6, 0)
    far_text(1)
    for slot in range(4, 8):
        for c in range(N_T):
            t_landed(slot, c)
    score(0)
    ring_on(2, 6, 1)
    score(1)
    image_part(1)
    ring_on(3, 5, 0)
    text_part(1, True)
    image_part(0)
    text_part(0, False)
    ring_on(3, 5, 1)
    score(2)
    image_part(2)
    sum_on(3, 0)
    sum_on(3, 1)
    sum_on(3, 2)
    sum_on(3, 3)
    ring_chunk(4, 0)
    ring_chunk(4, 1)
    score(3)
    image_part(3)
    sum_on(4, 0)
    sum_on(4, 1)
    sum_on(4, 2)
    sum_on(4, 3)
    sum_on(2, 0)
    text_part(2, False)
    sum_on(2, 1)
    text_part(3, False)
    sum_on(2, 2)
    sum_on(2, 3)
    to_sib(3)
    to_sib(2)
    to_sib(1)
    to_sib(0)
    sum_on(5, 0)
    from_sib(3)
    d_send(0, 3, 0, behind)
    d_send(1, 3, 1, ypart)
    sum_on(5, 1)
    from_sib(2)
    d_send(2, 2, 0, behind)
    sum_on(5, 2)
    from_sib(1)
    d_send(3, 1, 1, ypart)
    sum_on(5, 3)
    from_sib(0)
    sum_on(1, 0)
    sum_on(1, 1)
    d_add(1, 2, 1)
    d_send(4, 2, 1, behind)
    sum_on(1, 2)
    sum_on(1, 3)
    d_add(0, 1, 0)
    d_send(5, 1, 0, ypart)
    sum_on(6, 0)
    sum_on(6, 1)
    d_add(3, 0, 1)
    sum_on(6, 2)
    sum_on(6, 3)
    d_add(2, 0, 0)
    sum_on(7, 0)
    sum_on(7, 1)
    d_add(5, 0, 0)
    sum_on(7, 2)
    sum_on(7, 3)
    d_add(4, 0, 1)
    restore(raw_t, norm_t, pl.ds(0, rows), tgrad[pl.ds(0, rows), :])
    out = [pltpu.make_async_copy(raw_t, text_grad_ref, out_sem.at[0])]
    out[0].start()
    for copy in sent:
        copy.wait_send()
    mine = losses[:, pl.ds(7 * rows, rows)]
    for came in ends(0):
        landed(rloss.at[came], l_r.at[came])
        mine = mine + rloss[came, 0:1, :]
    loss_ref[...] = mine / (STEPS * rows * lax.axis_size("ing"))
    n = rows // N_RS
    for c in range(N_RS):
        at = pl.ds(c * n, n)
        value = part[pl.ds(7 * rows + c * n, n), :]
        for came in ends(c):
            landed(racc.at[came, at], rs_r.at[came, c])
            value = value + racc[came, at, :].astype(F32)
        restore(raw_i, norm_i, at, value)
        out.append(pltpu.make_async_copy(raw_i.at[at], image_grad_ref.at[at], out_sem.at[1 + c]))
        out[-1].start()
    for copy in out:
        copy.wait()


def finish(image_in_ref, text_in_ref, loss_in_ref, loss_ref, image_grad_ref, text_grad_ref):
    image_grad_ref[...] = image_in_ref[...]
    text_grad_ref[...] = text_in_ref[...]
    loss_ref[...] = loss_in_ref[0, :]


def on_device(image_emb, text_emb, logit_scale, logit_bias):
    rows, embed = image_emb.shape
    full, dma = RING * rows, pltpu.SemaphoreType.DMA
    wide, half = 2 * rows, rows // 2
    whole, far = pl.BlockSpec(memory_space=pltpu.VMEM), pl.BlockSpec(memory_space=pltpu.HBM)
    vmem = pltpu.VMEM
    loss, image_grad, text_grad = pl.pallas_call(
        kernel,
        out_shape=(
            jax.ShapeDtypeStruct((1, rows), F32),
            jax.ShapeDtypeStruct((rows, embed), F32),
            jax.ShapeDtypeStruct((rows, embed), F32),
        ),
        in_specs=[far, far, far, far],
        out_specs=(whole, far, far),
        scratch_shapes=[
            pltpu.SMEM((2, 1), F32),
            vmem((rows, embed), F32),
            vmem((rows, embed), F32),
            vmem((rows, 1), F32),
            vmem((rows, 1), F32),
            vmem((full, embed), BF16),
            vmem((full, embed), BF16),
            vmem((4, full, wide), BF16),
            vmem((full, embed), F32),
            vmem((full, embed), F32),
            vmem((RING + 1, rows, embed), BF16),
            vmem((7, rows, embed), BF16),
            vmem((RING + 1, 8, rows), F32),
            vmem((7, 8, rows), F32),
            vmem((1, full), F32),
            vmem((4, rows, embed), BF16),
            vmem((4, rows, embed), BF16),
            vmem((6, half, embed), BF16),
            vmem((6, half, embed), BF16),
            dma((N_AG + 3,)), dma((1 + N_RS,)),
            dma((7, N_AG)), dma((7, N_AG)),
            dma((8, N_T)), dma((7, N_T)),
            dma((7, N_RS)), dma((RING + 1, N_RS)),
            dma((7,)), dma((RING + 1,)),
            dma((4,)), dma((4,)),
            dma((6,)), dma((6,)),
        ],
        compiler_params=pltpu.CompilerParams(
            collective_id=0, has_side_effects=True, vmem_limit_bytes=56 * 2**20
        ),
        cost_estimate=pl.CostEstimate(
            flops=6 * full * full * embed, bytes_accessed=16 * rows * embed, transcendentals=3 * full * full
        ),
    )(image_emb, text_emb, logit_scale, logit_bias)
    n_cut = 2
    tile = pl.BlockSpec((rows // n_cut, embed), lambda n: (n, 0))
    return pl.pallas_call(
        finish,
        grid=(n_cut,),
        out_shape=(
            jax.ShapeDtypeStruct((rows,), F32),
            jax.ShapeDtypeStruct((rows, embed), F32),
            jax.ShapeDtypeStruct((rows, embed), F32),
        ),
        in_specs=[tile, tile, pl.BlockSpec((1, rows), lambda n: (0, 0))],
        out_specs=(pl.BlockSpec((rows,), lambda n: (0,)), tile, tile),
    )(image_grad, text_grad, loss)


def solution(mesh):
    placed = (P(("grp", "ing"), None), P(("grp", "ing"), None), P(), P())
    return jax.shard_map(
        on_device,
        mesh=mesh,
        in_specs=placed,
        out_specs=(P(("grp", "ing")), P(("grp", "ing"), None), P(("grp", "ing"), None)),
        check_vma=False,
    )
```

```python
import jax
import jax.numpy as jnp
from jax import lax
from jax.experimental import pallas as pl
from jax.experimental.pallas import tpu as pltpu
from jax.sharding import PartitionSpec as P

STEPS = 2
EPSILON = 1e-06
MESH = pl.DeviceIdType.MESH
F32, BF16 = jnp.float32, jnp.bfloat16

CORES, RING = 2, 8
N_AG = 4
N_T = 4
SLOT = {1: 0, 7: 1, 2: 2, 6: 3, 3: 4, 5: 5, 4: 6, 0: 7}
TURNS = (4, 4, 4, 4)
N_RS = len(TURNS)


def column_dot(left, right):
    return lax.dot_general(left, right, (((1,), (1,)), ((), ())), preferred_element_type=F32)


def row_norms(raw):
    return jnp.sqrt(jnp.sum(raw * raw, axis=1, keepdims=True) + EPSILON)


def kernel(
    image_ref, text_ref, scale_ref, bias_ref,
    loss_ref, image_grad_ref, text_grad_ref,
    scalars, raw_i, raw_t, norm_i, norm_t, img, txt, coef, part, tgrad, racc, sacc, rloss, sloss, losses,
    sib_out, sib_in, d_out, d_in,
    in_sem, ag_s, ag_r, t_r, f_s, rs_s, rs_r, l_s, l_r, sib_s, sib_r, d_s, d_r,
):
    rows, embed = raw_i.shape
    n_grp = lax.axis_size("grp")
    g, i = lax.axis_index("grp"), lax.axis_index("ing")
    core, z, y = i % CORES, (i // CORES) % RING, i // (CORES * RING)
    dz = 1 - 2 * core

    def device(group, y_, z_, core_):
        return (group, (y_ * RING + z_) * CORES + core_)

    nxt = device(g, y, lax.rem(z + dz + RING, RING), core)
    prv = device(g, y, lax.rem(z - dz + RING, RING), core)
    sib = device(g, y, z, 1 - core)
    ypart = device(g, 1 - y, z, core)
    ahead = device(lax.rem(g + 1, n_grp), 1 - y, z, core)
    behind = device(lax.rem(g + n_grp - 1, n_grp), 1 - y, z, core)

    barrier = pltpu.get_barrier_semaphore()
    for peer in (nxt, prv, sib, ypart, ahead, behind):
        pl.semaphore_signal(barrier, inc=1, device_id=peer, device_id_type=MESH)

    def fetch(src, dst, n):
        copy = pltpu.make_async_copy(src, dst, in_sem.at[n])
        copy.start()
        return copy

    n_ag = rows // N_AG
    fetch_i = [
        fetch(image_ref.at[pl.ds(c * n_ag, n_ag)], raw_i.at[pl.ds(c * n_ag, n_ag)], c)
        for c in range(N_AG)
    ]
    fetch_t = fetch(text_ref, raw_t, N_AG)
    fetch_s = [
        fetch(scale_ref, scalars.at[0], N_AG + 1), fetch(bias_ref, scalars.at[1], N_AG + 2)
    ]

    sent = []

    def send(src, dst, s_sem, r_sem, to):
        copy = pltpu.make_async_remote_copy(
            src_ref=src, dst_ref=dst, send_sem=s_sem, recv_sem=r_sem,
            device_id=to, device_id_type=MESH,
        )
        copy.start()
        sent.append(copy)

    def landed(dst, sem):
        pltpu.make_async_remote_copy(
            src_ref=dst, dst_ref=dst, send_sem=sem, recv_sem=sem,
            device_id=nxt, device_id_type=MESH,
        ).wait_recv()

    def img_rows(hop, c):
        n = rows // N_AG
        return img.at[pl.ds(SLOT[hop] * rows + c * n, n)]

    def ring_send(hop, to, c, peer):
        send(img_rows(hop, c), img_rows(to, c), ag_s.at[to - 1, c], ag_r.at[to - 1, c], peer)

    def ring_chunk(hop, c):
        landed(img_rows(hop, c), ag_r.at[hop - 1, c])
        if hop < RING // 2:
            ring_send(hop, hop + 1, c, nxt)
        elif hop > RING // 2 + 1:
            ring_send(hop, hop - 1, c, prv)

    def t_rows(slot, c):
        n = rows // N_T
        return txt.at[pl.ds(slot * rows + c * n, n)]

    def t_send(slot, c, to_slot, sem, to):
        send(t_rows(slot, c), t_rows(to_slot, c), f_s.at[sem, c], t_r.at[to_slot, c], to)

    def t_landed(slot, c):
        landed(t_rows(slot, c), t_r.at[slot, c])

    def normalize(raw_ref, norm_ref, low):
        raw = raw_ref[...]
        norms = row_norms(raw)
        norm_ref[...] = norms
        low[...] = (raw / norms).astype(BF16)

    def restore(raw_ref, norm_ref, grad_ref, at, unit_grad):
        norms = norm_ref[at, :]
        units = raw_ref[at, :] / norms
        grad = scale * unit_grad
        grad_ref[at, :] = (grad - units * jnp.sum(units * grad, axis=1, keepdims=True)) / norms

    wide = 2 * rows

    def images(u, lo=0, hi=2):
        return pl.ds((2 * u + lo) * rows, (hi - lo) * rows)

    def score(u, lo=0, hi=2):
        at, columns = images(u, lo, hi), pl.ds(lo * rows, (hi - lo) * rows)
        x = scale * column_dot(txt[...], img[at, :]) + bias
        e = jnp.exp(x)
        one = 1.0 + e
        inv = pl.reciprocal(one, approx=True)
        inv = inv * (2.0 - one * inv)
        loss = jnp.log(one) + (e - (one - 1.0)) * inv
        coef[u, :, columns] = (e * inv).astype(BF16)
        losses[:, at] = jnp.sum(loss, axis=0, keepdims=True)
        if (u, hi) == (3, 2):
            mine = (hi - lo - 1) * rows
            x = x[:rows, mine:]
            own = lax.broadcasted_iota(jnp.int32, x.shape, 0) == lax.broadcasted_iota(
                jnp.int32, x.shape, 1
            )
            m = jnp.exp(-jnp.abs(x))
            one_m = 1.0 + m
            pair = jnp.log(one_m) + (m - (one_m - 1.0)) / one_m + jnp.maximum(-x, 0.0)
            inv = inv[:rows, mine:]
            coef[u, :rows, rows:] = jnp.where(own, -inv, e[:rows, mine:] * inv).astype(BF16)
            loss = jnp.concatenate(
                [jnp.where(own, pair, loss[:rows, mine:]), loss[rows:, mine:]], axis=0
            )
            losses[:, pl.ds(7 * rows, rows)] = jnp.sum(loss, axis=0, keepdims=True)

    def image_part(u, lo=0, hi=2):
        part[images(u, lo, hi), :] = lax.dot_general(
            coef[u, :, lo * rows : hi * rows], txt[...], (((0,), (0,)), ((), ())),
            preferred_element_type=F32,
        )

    def text_part(u, first):
        add = jnp.dot(coef[u], img[images(u), :], preferred_element_type=F32)
        tgrad[...] = add if first else tgrad[...] + add

    def sum_on(hop, c):
        slot = SLOT[hop]
        to, peer = (hop + 1, nxt) if hop >= TURNS[c] else (hop - 1, prv)
        starts = hop in (TURNS[c], TURNS[c] - 1)
        n = rows // N_RS
        at = pl.ds(c * n, n)
        value = part[pl.ds(slot * rows + c * n, n), :]
        if not starts:
            landed(racc.at[hop, at], rs_r.at[hop, c])
            value = value + racc[hop, at, :].astype(F32)
        sacc[slot, at, :] = value.astype(BF16)
        send(sacc.at[slot, at], racc.at[to, at], rs_s.at[slot, c], rs_r.at[to, c], peer)
        if c == 0:
            mine = losses[:, pl.ds(slot * rows, rows)]
            if not starts:
                landed(rloss.at[hop], l_r.at[hop])
                mine = mine + rloss[hop, 0:1, :]
            sloss[slot] = jnp.broadcast_to(mine, (8, rows))
            send(sloss.at[slot], rloss.at[to], l_s.at[slot], l_r.at[to], peer)

    def ends(c):
        return (0, RING) if TURNS[c] > 1 else (RING,)

    half = rows // 2

    def to_sib(s):
        sib_out[s] = tgrad[pl.ds((4 + s) * rows, rows), :].astype(BF16)
        send(sib_out.at[s], sib_in.at[s], sib_s.at[s], sib_r.at[s], sib)

    def from_sib(s):
        landed(sib_in.at[s], sib_r.at[s])
        at = pl.ds(s * rows, rows)
        tgrad[at, :] = tgrad[at, :] + sib_in[s].astype(F32)

    def t_half(s, h):
        return pl.ds(s * rows + h * half, half)

    def d_send(m, s, h, to):
        d_out[m] = tgrad[t_half(s, h), :].astype(BF16)
        send(d_out.at[m], d_in.at[m], d_s.at[m], d_r.at[m], to)

    def d_add(m, s, h):
        landed(d_in.at[m], d_r.at[m])
        at = t_half(s, h)
        tgrad[at, :] = tgrad[at, :] + d_in[m].astype(F32)

    for c in range(N_AG):
        fetch_i[c].wait()
        at = pl.ds(c * n_ag, n_ag)
        normalize(raw_i.at[at], norm_i.at[at], img_rows(0, c))
        if c == 0:
            pl.semaphore_wait(barrier, 6)
        ring_send(0, 1, c, nxt)
        ring_send(0, 7, c, prv)
    fetch_t.wait()
    normalize(raw_t, norm_t, txt.at[pl.ds(0, rows)])
    for c in range(N_T):
        t_send(0, c, 1, 1, ypart)
        t_send(0, (c + 2) % N_T, 2, 0, ahead)
    for c in range(N_T):
        t_send(0, c, 4, 2, sib)
    for copy in fetch_s:
        copy.wait()
    scale, bias = scalars[0, 0], scalars[1, 0]

    def ring_on(hop, back, c):
        ring_chunk(hop, c)
        ring_chunk(back, c)

    def partner_text(c):
        t_landed(1, c)
        if c < 2:
            t_send(1, c, 3, 3, ahead)
        t_send(1, c, 5, 4, sib)

    def behind_text(c):
        t_landed(2, c)
        if c >= 2:
            t_send(2, c, 3, 3, ypart)
        t_send(2, c, 6, 5, sib)

    def far_text(c):
        t_landed(3, c)
        t_send(3, c, 7, 6, sib)

    partner_text(0)
    behind_text(2)
    partner_text(1)
    ring_on(1, 7, 0)
    ring_on(1, 7, 1)
    behind_text(3)
    partner_text(2)
    behind_text(0)
    partner_text(3)
    ring_on(1, 7, 2)
    ring_on(1, 7, 3)
    behind_text(1)
    far_text(2)
    far_text(0)
    far_text(3)
    ring_on(2, 6, 0)
    ring_on(2, 6, 1)
    far_text(1)
    for slot in range(4, 8):
        for c in range(N_T):
            t_landed(slot, c)
    score(0)
    ring_on(2, 6, 2)
    ring_on(2, 6, 3)
    score(1)
    image_part(1)
    ring_on(3, 5, 0)
    ring_on(3, 5, 1)
    text_part(1, True)
    image_part(0)
    text_part(0, False)
    ring_on(3, 5, 2)
    ring_on(3, 5, 3)
    score(2, 0, 1)
    image_part(2, 0, 1)
    sum_on(3, 0)
    sum_on(3, 1)
    sum_on(3, 2)
    sum_on(3, 3)
    score(2, 1, 2)
    ring_chunk(4, 0)
    ring_chunk(4, 1)
    ring_chunk(4, 2)
    ring_chunk(4, 3)
    score(3, 0, 1)
    image_part(3, 0, 1)
    sum_on(4, 0)
    sum_on(4, 1)
    sum_on(4, 2)
    sum_on(4, 3)
    score(3, 1, 2)
    text_part(2, False)
    sum_on(2, 0)
    sum_on(2, 1)
    sum_on(2, 2)
    sum_on(2, 3)
    text_part(3, False)
    image_part(2, 1, 2)
    image_part(3, 1, 2)
    to_sib(3)
    to_sib(2)
    to_sib(1)
    to_sib(0)
    sum_on(5, 0)
    from_sib(3)
    d_send(0, 3, 0, behind)
    d_send(1, 3, 1, ypart)
    sum_on(5, 1)
    from_sib(2)
    d_send(2, 2, 0, behind)
    sum_on(5, 2)
    from_sib(1)
    d_send(3, 1, 1, ypart)
    sum_on(5, 3)
    from_sib(0)
    sum_on(1, 0)
    sum_on(1, 1)
    d_add(1, 2, 1)
    d_send(4, 2, 1, behind)
    sum_on(1, 2)
    sum_on(1, 3)
    d_add(0, 1, 0)
    d_send(5, 1, 0, ypart)
    sum_on(6, 0)
    sum_on(6, 1)
    d_add(3, 0, 1)
    sum_on(6, 2)
    sum_on(6, 3)
    d_add(2, 0, 0)
    sum_on(7, 0)
    sum_on(7, 1)
    d_add(5, 0, 0)
    sum_on(7, 2)
    sum_on(7, 3)
    d_add(4, 0, 1)
    restore(raw_t, norm_t, text_grad_ref, pl.ds(0, rows), tgrad[pl.ds(0, rows), :])
    for copy in sent:
        copy.wait_send()
    mine = losses[:, pl.ds(7 * rows, rows)]
    for came in ends(0):
        landed(rloss.at[came], l_r.at[came])
        mine = mine + rloss[came, 0:1, :]
    loss_ref[...] = mine[0, :] / (STEPS * rows * lax.axis_size("ing"))
    n = rows // N_RS
    for c in range(N_RS):
        at = pl.ds(c * n, n)
        value = part[pl.ds(7 * rows + c * n, n), :]
        for came in ends(c):
            landed(racc.at[came, at], rs_r.at[came, c])
            value = value + racc[came, at, :].astype(F32)
        restore(raw_i, norm_i, image_grad_ref, at, value)


def finish(image_in_ref, text_in_ref, loss_in_ref, loss_ref, image_grad_ref, text_grad_ref, sem):
    image = pltpu.make_async_copy(image_in_ref, image_grad_ref, sem.at[0])
    text = pltpu.make_async_copy(text_in_ref, text_grad_ref, sem.at[1])
    image.start()
    text.start()
    loss_ref[...] = loss_in_ref[0, :]
    image.wait()
    text.wait()


def on_device(image_emb, text_emb, logit_scale, logit_bias):
    rows, embed = image_emb.shape
    full, dma = RING * rows, pltpu.SemaphoreType.DMA
    wide, half = 2 * rows, rows // 2
    whole, far = pl.BlockSpec(memory_space=pltpu.VMEM), pl.BlockSpec(memory_space=pltpu.HBM)
    vmem = pltpu.VMEM
    loss, image_grad, text_grad = pl.pallas_call(
        kernel,
        out_shape=(vmem((rows,), F32), vmem((rows, embed), F32), vmem((rows, embed), F32)),
        in_specs=[far, far, far, far],
        out_specs=(whole, whole, whole),
        scratch_shapes=[
            pltpu.SMEM((2, 1), F32),
            vmem((rows, embed), F32),
            vmem((rows, embed), F32),
            vmem((rows, 1), F32),
            vmem((rows, 1), F32),
            vmem((full, embed), BF16),
            vmem((full, embed), BF16),
            vmem((4, full, wide), BF16),
            vmem((full, embed), F32),
            vmem((full, embed), F32),
            vmem((RING + 1, rows, embed), BF16),
            vmem((7, rows, embed), BF16),
            vmem((RING + 1, 8, rows), F32),
            vmem((7, 8, rows), F32),
            vmem((1, full), F32),
            vmem((4, rows, embed), BF16),
            vmem((4, rows, embed), BF16),
            vmem((6, half, embed), BF16),
            vmem((6, half, embed), BF16),
            dma((N_AG + 3,)),
            dma((7, N_AG)), dma((7, N_AG)),
            dma((8, N_T)), dma((7, N_T)),
            dma((7, N_RS)), dma((RING + 1, N_RS)),
            dma((7,)), dma((RING + 1,)),
            dma((4,)), dma((4,)),
            dma((6,)), dma((6,)),
        ],
        compiler_params=pltpu.CompilerParams(
            collective_id=0, has_side_effects=True, vmem_limit_bytes=56 * 2**20
        ),
        cost_estimate=pl.CostEstimate(
            flops=6 * full * full * embed, bytes_accessed=16 * rows * embed, transcendentals=3 * full * full
        ),
    )(image_emb, text_emb, logit_scale, logit_bias)
    return loss, image_grad, text_grad


def solution(mesh):
    placed = (P(("grp", "ing"), None), P(("grp", "ing"), None), P(), P())
    return jax.shard_map(
        on_device,
        mesh=mesh,
        in_specs=placed,
        out_specs=(P(("grp", "ing")), P(("grp", "ing"), None), P(("grp", "ing"), None)),
        check_vma=False,
    )
```

```python
import jax
import jax.numpy as jnp
from jax import lax
from jax.experimental import pallas as pl
from jax.experimental.pallas import tpu as pltpu
from jax.sharding import PartitionSpec as P

STEPS = 2
EPSILON = 1e-06
MESH = pl.DeviceIdType.MESH
F32, BF16 = jnp.float32, jnp.bfloat16

CORES, RING = 2, 8
N_AG = 4
N_T = 4
SLOT = {1: 0, 7: 1, 2: 2, 6: 3, 3: 4, 5: 5, 4: 6, 0: 7}
TURNS = (4, 4, 4, 4)
N_RS = len(TURNS)


def column_dot(left, right):
    return lax.dot_general(left, right, (((1,), (1,)), ((), ())), preferred_element_type=F32)


def row_norms(raw):
    return jnp.sqrt(jnp.sum(raw * raw, axis=1, keepdims=True) + EPSILON)


def kernel(
    image_ref, text_ref, scale_ref, bias_ref,
    loss_ref, image_grad_ref, text_grad_ref,
    scalars, raw_i, raw_t, norm_i, norm_t, img, txt, coef, part, tgrad, racc, sacc, rloss, sloss, losses,
    sib_out, sib_in, d_out, d_in,
    in_sem, ag_s, ag_r, t_r, f_s, rs_s, rs_r, l_s, l_r, sib_s, sib_r, d_s, d_r,
):
    rows, embed = raw_i.shape
    n_grp = lax.axis_size("grp")
    g, i = lax.axis_index("grp"), lax.axis_index("ing")
    core, z, y = i % CORES, (i // CORES) % RING, i // (CORES * RING)
    dz = 1 - 2 * core

    def device(group, y_, z_, core_):
        return (group, (y_ * RING + z_) * CORES + core_)

    nxt = device(g, y, lax.rem(z + dz + RING, RING), core)
    prv = device(g, y, lax.rem(z - dz + RING, RING), core)
    sib = device(g, y, z, 1 - core)
    ypart = device(g, 1 - y, z, core)
    ahead = device(lax.rem(g + 1, n_grp), 1 - y, z, core)
    behind = device(lax.rem(g + n_grp - 1, n_grp), 1 - y, z, core)

    barrier = pltpu.get_barrier_semaphore()
    for peer in (nxt, prv, sib, ypart, ahead, behind):
        pl.semaphore_signal(barrier, inc=1, device_id=peer, device_id_type=MESH)

    def fetch(src, dst, n):
        copy = pltpu.make_async_copy(src, dst, in_sem.at[n])
        copy.start()
        return copy

    n_ag = rows // N_AG
    fetch_i = [
        fetch(image_ref.at[pl.ds(c * n_ag, n_ag)], raw_i.at[pl.ds(c * n_ag, n_ag)], c)
        for c in range(N_AG)
    ]
    fetch_t = fetch(text_ref, raw_t, N_AG)
    fetch_s = [
        fetch(scale_ref, scalars.at[0], N_AG + 1), fetch(bias_ref, scalars.at[1], N_AG + 2)
    ]

    sent = []

    def send(src, dst, s_sem, r_sem, to):
        copy = pltpu.make_async_remote_copy(
            src_ref=src, dst_ref=dst, send_sem=s_sem, recv_sem=r_sem,
            device_id=to, device_id_type=MESH,
        )
        copy.start()
        sent.append(copy)

    def landed(dst, sem):
        pltpu.make_async_remote_copy(
            src_ref=dst, dst_ref=dst, send_sem=sem, recv_sem=sem,
            device_id=nxt, device_id_type=MESH,
        ).wait_recv()

    def img_rows(hop, c):
        n = rows // N_AG
        return img.at[pl.ds(SLOT[hop] * rows + c * n, n)]

    def ring_send(hop, to, c, peer):
        send(img_rows(hop, c), img_rows(to, c), ag_s.at[to - 1, c], ag_r.at[to - 1, c], peer)

    def ring_chunk(hop, c):
        landed(img_rows(hop, c), ag_r.at[hop - 1, c])
        if hop < RING // 2:
            ring_send(hop, hop + 1, c, nxt)
        elif hop > RING // 2 + 1:
            ring_send(hop, hop - 1, c, prv)

    def t_rows(slot, c):
        n = rows // N_T
        return txt.at[pl.ds(slot * rows + c * n, n)]

    def t_send(slot, c, to_slot, sem, to):
        send(t_rows(slot, c), t_rows(to_slot, c), f_s.at[sem, c], t_r.at[to_slot, c], to)

    def t_landed(slot, c):
        landed(t_rows(slot, c), t_r.at[slot, c])

    def normalize(raw_ref, norm_ref, low):
        raw = raw_ref[...]
        norms = row_norms(raw)
        norm_ref[...] = norms
        low[...] = (raw / norms).astype(BF16)

    def restore(raw_ref, norm_ref, grad_ref, at, unit_grad):
        norms = norm_ref[at, :]
        units = raw_ref[at, :] / norms
        grad = scale * unit_grad
        grad_ref[at, :] = (grad - units * jnp.sum(units * grad, axis=1, keepdims=True)) / norms

    wide = 2 * rows

    def images(u, lo=0, hi=2):
        return pl.ds((2 * u + lo) * rows, (hi - lo) * rows)

    def score(u, lo=0, hi=2):
        at, columns = images(u, lo, hi), pl.ds(lo * rows, (hi - lo) * rows)
        x = scale * column_dot(txt[...], img[at, :]) + bias
        e = jnp.exp(x)
        one = 1.0 + e
        inv = pl.reciprocal(one, approx=True)
        inv = inv * (2.0 - one * inv)
        loss = jnp.log(one) + (e - (one - 1.0)) * inv
        coef[u, :, columns] = (e * inv).astype(BF16)
        losses[:, at] = jnp.sum(loss, axis=0, keepdims=True)
        if (u, hi) == (3, 2):
            mine = (hi - lo - 1) * rows
            x = x[:rows, mine:]
            own = lax.broadcasted_iota(jnp.int32, x.shape, 0) == lax.broadcasted_iota(
                jnp.int32, x.shape, 1
            )
            m = jnp.exp(-jnp.abs(x))
            one_m = 1.0 + m
            pair = jnp.log(one_m) + (m - (one_m - 1.0)) / one_m + jnp.maximum(-x, 0.0)
            inv = inv[:rows, mine:]
            coef[u, :rows, rows:] = jnp.where(own, -inv, e[:rows, mine:] * inv).astype(BF16)
            loss = jnp.concatenate(
                [jnp.where(own, pair, loss[:rows, mine:]), loss[rows:, mine:]], axis=0
            )
            losses[:, pl.ds(7 * rows, rows)] = jnp.sum(loss, axis=0, keepdims=True)

    def image_part(u, lo=0, hi=2):
        part[images(u, lo, hi), :] = lax.dot_general(
            coef[u, :, lo * rows : hi * rows], txt[...], (((0,), (0,)), ((), ())),
            preferred_element_type=F32,
        )

    def text_part(u, first):
        add = jnp.dot(coef[u], img[images(u), :], preferred_element_type=F32)
        tgrad[...] = add if first else tgrad[...] + add

    def sum_on(hop, c):
        slot = SLOT[hop]
        to, peer = (hop + 1, nxt) if hop >= TURNS[c] else (hop - 1, prv)
        starts = hop in (TURNS[c], TURNS[c] - 1)
        n = rows // N_RS
        at = pl.ds(c * n, n)
        value = part[pl.ds(slot * rows + c * n, n), :]
        if not starts:
            landed(racc.at[hop, at], rs_r.at[hop, c])
            value = value + racc[hop, at, :].astype(F32)
        sacc[slot, at, :] = value.astype(BF16)
        send(sacc.at[slot, at], racc.at[to, at], rs_s.at[slot, c], rs_r.at[to, c], peer)
        if c == 0:
            mine = losses[:, pl.ds(slot * rows, rows)]
            if not starts:
                landed(rloss.at[hop], l_r.at[hop])
                mine = mine + rloss[hop, 0:1, :]
            sloss[slot] = jnp.broadcast_to(mine, (8, rows))
            send(sloss.at[slot], rloss.at[to], l_s.at[slot], l_r.at[to], peer)

    def ends(c):
        return (0, RING) if TURNS[c] > 1 else (RING,)

    half = rows // 2

    def to_sib(s):
        sib_out[s] = tgrad[pl.ds((4 + s) * rows, rows), :].astype(BF16)
        send(sib_out.at[s], sib_in.at[s], sib_s.at[s], sib_r.at[s], sib)

    def from_sib(s):
        landed(sib_in.at[s], sib_r.at[s])
        at = pl.ds(s * rows, rows)
        tgrad[at, :] = tgrad[at, :] + sib_in[s].astype(F32)

    def t_half(s, h):
        return pl.ds(s * rows + h * half, half)

    def d_send(m, s, h, to):
        d_out[m] = tgrad[t_half(s, h), :].astype(BF16)
        send(d_out.at[m], d_in.at[m], d_s.at[m], d_r.at[m], to)

    def d_add(m, s, h):
        landed(d_in.at[m], d_r.at[m])
        at = t_half(s, h)
        tgrad[at, :] = tgrad[at, :] + d_in[m].astype(F32)

    for c in range(N_AG):
        fetch_i[c].wait()
        at = pl.ds(c * n_ag, n_ag)
        normalize(raw_i.at[at], norm_i.at[at], img_rows(0, c))
        if c == 0:
            pl.semaphore_wait(barrier, 6)
        ring_send(0, 1, c, nxt)
        ring_send(0, 7, c, prv)
    fetch_t.wait()
    normalize(raw_t, norm_t, txt.at[pl.ds(0, rows)])
    for c in range(N_T):
        t_send(0, c, 1, 1, ypart)
        t_send(0, (c + 2) % N_T, 2, 0, ahead)
    for c in range(N_T):
        t_send(0, c, 4, 2, sib)
    for copy in fetch_s:
        copy.wait()
    scale, bias = scalars[0, 0], scalars[1, 0]

    def ring_on(hop, back, c):
        ring_chunk(hop, c)
        ring_chunk(back, c)

    def partner_text(c):
        t_landed(1, c)
        if c < 2:
            t_send(1, c, 3, 3, ahead)
        t_send(1, c, 5, 4, sib)

    def behind_text(c):
        t_landed(2, c)
        if c >= 2:
            t_send(2, c, 3, 3, ypart)
        t_send(2, c, 6, 5, sib)

    def far_text(c):
        t_landed(3, c)
        t_send(3, c, 7, 6, sib)

    partner_text(0)
    behind_text(2)
    partner_text(1)
    ring_on(1, 7, 0)
    ring_on(1, 7, 1)
    behind_text(3)
    partner_text(2)
    behind_text(0)
    partner_text(3)
    ring_on(1, 7, 2)
    ring_on(1, 7, 3)
    behind_text(1)
    far_text(2)
    far_text(0)
    far_text(3)
    ring_on(2, 6, 0)
    ring_on(2, 6, 1)
    far_text(1)
    for slot in range(4, 8):
        for c in range(N_T):
            t_landed(slot, c)
    score(0)
    ring_on(2, 6, 2)
    ring_on(2, 6, 3)
    score(1)
    image_part(1)
    ring_on(3, 5, 0)
    ring_on(3, 5, 1)
    image_part(0)
    ring_on(3, 5, 2)
    ring_on(3, 5, 3)
    score(2, 0, 1)
    image_part(2, 0, 1)
    sum_on(3, 0)
    sum_on(3, 1)
    sum_on(3, 2)
    sum_on(3, 3)
    score(2, 1, 2)
    text_part(1, True)
    ring_chunk(4, 0)
    ring_chunk(4, 1)
    ring_chunk(4, 2)
    ring_chunk(4, 3)
    score(3, 0, 1)
    image_part(3, 0, 1)
    sum_on(4, 0)
    sum_on(4, 1)
    sum_on(4, 2)
    sum_on(4, 3)
    score(3, 1, 2)
    text_part(0, False)
    sum_on(2, 0)
    sum_on(2, 1)
    sum_on(2, 2)
    sum_on(2, 3)
    text_part(2, False)
    image_part(2, 1, 2)
    text_part(3, False)
    image_part(3, 1, 2)
    to_sib(3)
    to_sib(2)
    to_sib(1)
    to_sib(0)
    sum_on(5, 0)
    from_sib(3)
    d_send(0, 3, 0, behind)
    d_send(1, 3, 1, ypart)
    sum_on(5, 1)
    from_sib(2)
    d_send(2, 2, 0, behind)
    sum_on(5, 2)
    from_sib(1)
    d_send(3, 1, 1, ypart)
    sum_on(5, 3)
    from_sib(0)
    sum_on(1, 0)
    sum_on(1, 1)
    d_add(1, 2, 1)
    d_send(4, 2, 1, behind)
    sum_on(1, 2)
    sum_on(1, 3)
    d_add(0, 1, 0)
    d_send(5, 1, 0, ypart)
    sum_on(6, 0)
    sum_on(6, 1)
    d_add(3, 0, 1)
    sum_on(6, 2)
    sum_on(6, 3)
    d_add(2, 0, 0)
    sum_on(7, 0)
    sum_on(7, 1)
    d_add(5, 0, 0)
    sum_on(7, 2)
    sum_on(7, 3)
    d_add(4, 0, 1)
    restore(raw_t, norm_t, text_grad_ref, pl.ds(0, rows), tgrad[pl.ds(0, rows), :])
    for copy in sent:
        copy.wait_send()
    mine = losses[:, pl.ds(7 * rows, rows)]
    for came in ends(0):
        landed(rloss.at[came], l_r.at[came])
        mine = mine + rloss[came, 0:1, :]
    loss_ref[...] = mine[0, :] / (STEPS * rows * lax.axis_size("ing"))
    n = rows // N_RS
    for c in range(N_RS):
        at = pl.ds(c * n, n)
        value = part[pl.ds(7 * rows + c * n, n), :]
        for came in ends(c):
            landed(racc.at[came, at], rs_r.at[came, c])
            value = value + racc[came, at, :].astype(F32)
        restore(raw_i, norm_i, image_grad_ref, at, value)


def finish(image_in_ref, text_in_ref, loss_in_ref, loss_ref, image_grad_ref, text_grad_ref, sem):
    image = pltpu.make_async_copy(image_in_ref, image_grad_ref, sem.at[0])
    text = pltpu.make_async_copy(text_in_ref, text_grad_ref, sem.at[1])
    image.start()
    text.start()
    loss_ref[...] = loss_in_ref[0, :]
    image.wait()
    text.wait()


def on_device(image_emb, text_emb, logit_scale, logit_bias):
    rows, embed = image_emb.shape
    full, dma = RING * rows, pltpu.SemaphoreType.DMA
    wide, half = 2 * rows, rows // 2
    whole, far = pl.BlockSpec(memory_space=pltpu.VMEM), pl.BlockSpec(memory_space=pltpu.HBM)
    vmem = pltpu.VMEM
    loss, image_grad, text_grad = pl.pallas_call(
        kernel,
        out_shape=(vmem((rows,), F32), vmem((rows, embed), F32), vmem((rows, embed), F32)),
        in_specs=[far, far, far, far],
        out_specs=(whole, whole, whole),
        scratch_shapes=[
            pltpu.SMEM((2, 1), F32),
            vmem((rows, embed), F32),
            vmem((rows, embed), F32),
            vmem((rows, 1), F32),
            vmem((rows, 1), F32),
            vmem((full, embed), BF16),
            vmem((full, embed), BF16),
            vmem((4, full, wide), BF16),
            vmem((full, embed), F32),
            vmem((full, embed), F32),
            vmem((RING + 1, rows, embed), BF16),
            vmem((7, rows, embed), BF16),
            vmem((RING + 1, 8, rows), F32),
            vmem((7, 8, rows), F32),
            vmem((1, full), F32),
            vmem((4, rows, embed), BF16),
            vmem((4, rows, embed), BF16),
            vmem((6, half, embed), BF16),
            vmem((6, half, embed), BF16),
            dma((N_AG + 3,)),
            dma((7, N_AG)), dma((7, N_AG)),
            dma((8, N_T)), dma((7, N_T)),
            dma((7, N_RS)), dma((RING + 1, N_RS)),
            dma((7,)), dma((RING + 1,)),
            dma((4,)), dma((4,)),
            dma((6,)), dma((6,)),
        ],
        compiler_params=pltpu.CompilerParams(
            collective_id=0, has_side_effects=True, vmem_limit_bytes=56 * 2**20
        ),
        cost_estimate=pl.CostEstimate(
            flops=6 * full * full * embed, bytes_accessed=16 * rows * embed, transcendentals=3 * full * full
        ),
    )(image_emb, text_emb, logit_scale, logit_bias)
    return loss, image_grad, text_grad


def solution(mesh):
    placed = (P(("grp", "ing"), None), P(("grp", "ing"), None), P(), P())
    return jax.shard_map(
        on_device,
        mesh=mesh,
        in_specs=placed,
        out_specs=(P(("grp", "ing")), P(("grp", "ing"), None), P(("grp", "ing"), None)),
        check_vma=False,
    )
```
